32 devices in a mesh: expert: 16 (over z, x, core), replica: 2 (over y).
Axes of the slice: x: 2, y: 2, z: 4, core: 2. Of those that a mesh axis runs over, the one named last changes fastest.
Arguments:
- tokens: bfloat16 [2048, 2560], P('expert'), may hold values from -6 to 6
- expert_ids: int32 [2048, 6], P('expert'), may hold values from 0 to 15, all different within a row; in each aligned block of 128 rows (0 to 127, 128 to 255, ...) at most 64 rows name the same one
- route_weights: float32 [2048, 6], P('expert'), may hold values from 0.05 to 0.5
- w_gate: bfloat16 [16, 2560, 1536], P('expert', None, 'replica'), may hold values from -0.125 to 0.125
- w_up: bfloat16 [16, 2560, 1536], P('expert', None, 'replica'), may hold values from -0.125 to 0.125
- w_down: bfloat16 [16, 1536, 2560], P('expert', 'replica'), may hold values from -0.15625 to 0.15625
- cotangent: bfloat16 [2048, 2560], P('expert'), may hold values from -6 to 6
Outputs:
- mixed: bfloat16 [2048, 2560], P('expert', 'replica')
- tokens_grad: bfloat16 [2048, 2560], P('expert', 'replica')
The draws below stay inside these ranges and needn't reach their ends.
Inputs may be any that keep to these rules, and one draw needn't show every extreme that they name: `expert_ids`: each row names 6 different experts. In each aligned block of 128 rows no expert is named by more than 64 rows, a bound that some block reaches.
All inputs are finite; a program needn't handle non-finite values.
Results may differ from the reference program's by a relative error of at most 0.0064.
Values may be sent and summed in bfloat16 or wider, within the bound.
A program may use at most 128 MiB of HBM per device.

```python
import math
import jax
import jax.numpy as jnp
import numpy as np
from jax import lax

D = 2560
FF = 1536
TOP = 6
TOK_DEV = 128
EXPERTS = 16
CAP = 64
TOKENS = 2048


def shard_levels(stream_key, extent, split, smallest, top_value):
    gain, own = 1.0, jax.random.fold_in(stream_key, 6)
    for axis_at, shards_of in split:
        draws = jnp.exp(jax.random.uniform(jax.random.fold_in(own, axis_at), (shards_of,), jnp.float32, smallest / len(split), top_value / len(split)))
        gain = gain * jnp.repeat(draws, extent[axis_at] // shards_of).reshape([-1 if axis == axis_at else 1 for axis in range(len(extent))])
    return gain


def shared_out(rng, own, number, rows, amount, top, reach, lean):
    order = jax.random.permutation(rng, amount)
    heavy_load, common = shares(amount, rows * top, reach, lean, True), shares(amount, rows * top, reach, lean, False)
    places = jnp.arange(amount)

    def named(tallies, offset_by):
        used = int((tallies > 0).sum())
        fixed = max(1, used // 4)
        shifted = fixed + (places - fixed + offset_by * (used - fixed)) % max(1, amount - fixed)
        return jnp.zeros((amount,), jnp.int32).at[order[jnp.where(places < fixed, places, shifted)]].set(jnp.asarray(tallies, jnp.int32))

    tallies = jnp.where(number % 4 == 0, named(heavy_load, number // 4), named(common, number - number // 4 - 1))
    mixed = jax.random.permutation(jax.random.fold_in(own, 3), amount)
    giver, taker = mixed[0:amount // 2 * 2:2], mixed[1:amount // 2 * 2:2]
    margin = jnp.minimum(tallies[giver] - 1, reach - tallies[taker]) // 2
    margin = jnp.where((giver == order[0]) | (taker == order[0]) | (tallies[taker] == 0), 0, jnp.maximum(margin, 0))
    shifted = jax.random.randint(jax.random.fold_in(own, 4), (amount // 2,), 0, 1 << 20) % (margin + 1)
    tallies = tallies.at[giver].add(-shifted).at[taker].add(shifted)
    labels = jnp.searchsorted(jnp.cumsum(tallies), jnp.arange(rows * top), side="right").astype(jnp.int32)
    listing = labels.reshape(top, rows).T
    listing = listing[jax.random.permutation(jax.random.fold_in(own, 1), rows)]
    offset_by = jax.random.randint(jax.random.fold_in(own, 2), (rows, 1), 0, top)
    return jnp.take_along_axis(listing, (jnp.arange(top)[None, :] + offset_by) % top, axis=1)


def shares(number_of, total, reach, skew, full):
    weights = [(1 << 20) // math.isqrt(grade ** skew) + 1 for grade in range(1, number_of + 1)]
    largest = reach if full else min(reach, max(-(-total // number_of), total * weights[0] // sum(weights)))
    least = 1 if total - largest >= number_of - 1 else 0
    holding, rest = [largest] + [least] * (number_of - 1), total - largest - least * (number_of - 1)
    while rest > 0:
        movable = [i for i in range(1, number_of) if holding[i] < largest] or [i for i in range(1, number_of) if holding[i] < reach]
        whole, budget = sum([weights[i] for i in movable]), rest
        for i in movable:
            addition = min(reach - holding[i], max(1, budget * weights[i] // whole), rest)
            holding[i] = holding[i] + addition
            rest = rest - addition
    return np.array(holding)


def bell_draw(key, dims, width, bound, shards=(), kind=jnp.bfloat16):
    array = width * jax.random.normal(key, dims, jnp.float32)
    if shards:
        array = array * shard_levels(key, dims, shards, -0.22, 0.18)
    return jnp.clip(array, -bound, bound).astype(kind)


def setup_inputs(seed: int = 0) -> dict:
    arg_keys = jax.random.split(jax.random.key(seed), 8)
    tokens = bell_draw(arg_keys[0], (TOKENS, D), 1.0, 6.0, ((0, 16),))
    expert_ids_keys = jax.random.split(jax.random.fold_in(arg_keys[1], 1), TOKENS // TOK_DEV)
    expert_ids_turns = jax.random.permutation(jax.random.fold_in(arg_keys[1], 3), TOKENS // TOK_DEV)
    expert_ids = jax.vmap(lambda own, number: shared_out(jax.random.fold_in(arg_keys[1], 2), own, number, TOK_DEV, EXPERTS, TOP, CAP, 2))(expert_ids_keys, expert_ids_turns).reshape((TOKENS, TOP))
    route_weights = jnp.clip(0.05 + 0.45 * jax.random.uniform(arg_keys[2], (TOKENS, TOP), jnp.float32) ** shard_levels(arg_keys[2], (TOKENS, TOP), ((0, 16),), -0.2, 0.2), 0.05, 0.5)
    w_gate = bell_draw(arg_keys[3], (EXPERTS, D, FF), D ** -0.5, 0.125, ((0, 16), (2, 2)))
    w_up = bell_draw(arg_keys[4], (EXPERTS, D, FF), D ** -0.5, 0.125, ((0, 16), (2, 2)))
    w_down = bell_draw(arg_keys[5], (EXPERTS, FF, D), FF ** -0.5, 0.15625, ((0, 16), (1, 2)))
    cotangent = bell_draw(arg_keys[6], (TOKENS, D), 1.0, 6.0, ((0, 16),))
    return {"tokens": tokens, "expert_ids": expert_ids, "route_weights": route_weights, "w_gate": w_gate, "w_up": w_up, "w_down": w_down, "cotangent": cotangent}


def reference(tokens, expert_ids, route_weights, w_gate, w_up, w_down, cotangent):
    flat_ids = expert_ids.reshape(-1)
    flat_weights = route_weights.reshape(-1)
    limit = EXPERTS * CAP

    def per_expert(carry, expert):
        mixed_acc, grad_acc = carry
        chosen = flat_ids == expert
        taken = jnp.nonzero(chosen, size=limit, fill_value=0)[0].astype(jnp.int32)
        count = jnp.sum(chosen.astype(jnp.int32))
        valid = (jnp.arange(limit, dtype=jnp.int32) < count).astype(jnp.float32)
        token_rows = (taken // TOP).astype(jnp.int32)
        weight = flat_weights[taken]
        rows = tokens[token_rows]
        gate_w = w_gate[expert]
        up_w = w_up[expert]
        down_w = w_down[expert]
        gate = jnp.dot(rows, gate_w, preferred_element_type=jnp.float32)
        up = jnp.dot(rows, up_w, preferred_element_type=jnp.float32)
        sig = jax.nn.sigmoid(gate)
        act = gate * sig
        hidden = (act * up).astype(jnp.bfloat16)
        expert_out = jnp.dot(hidden, down_w, preferred_element_type=jnp.float32).astype(jnp.bfloat16)
        contrib = expert_out.astype(jnp.float32) * (weight * valid)[:, None]
        mixed_acc = mixed_acc.at[token_rows].add(contrib)
        slot_grad = (cotangent[token_rows].astype(jnp.float32) * weight[:, None]).astype(jnp.bfloat16)
        hidden_grad = jnp.dot(slot_grad, down_w.T, preferred_element_type=jnp.float32)
        gate_grad = (hidden_grad * up * sig * (1.0 + gate * (1.0 - sig))).astype(jnp.bfloat16)
        up_grad = (hidden_grad * act).astype(jnp.bfloat16)
        slot_input = jnp.dot(gate_grad, gate_w.T, preferred_element_type=jnp.float32)
        slot_input = slot_input + jnp.dot(up_grad, up_w.T, preferred_element_type=jnp.float32)
        slot_input = slot_input.astype(jnp.bfloat16).astype(jnp.float32) * valid[:, None]
        grad_acc = grad_acc.at[token_rows].add(slot_input)
        return (mixed_acc, grad_acc), None

    start = (jnp.zeros(tokens.shape, jnp.float32), jnp.zeros(tokens.shape, jnp.float32))
    (mixed_acc, grad_acc), _ = lax.scan(per_expert, start, jnp.arange(EXPERTS, dtype=jnp.int32))
    return mixed_acc.astype(jnp.bfloat16), grad_acc.astype(jnp.bfloat16)
```

```python
import jax
import jax.numpy as jnp
from jax import lax
from jax.sharding import PartitionSpec as P

BF16 = jnp.bfloat16
F32 = jnp.float32


def slots_of(chosen, capacity):
    count = chosen.shape[-1]
    earlier = (jnp.arange(count)[:, None] < jnp.arange(count)[None, :]).astype(BF16)
    slot = jnp.dot(chosen.astype(BF16), earlier, preferred_element_type=F32).astype(jnp.int32)
    at_slot = slot[..., None, :] == jnp.arange(capacity, dtype=jnp.int32)[:, None]
    return (at_slot & chosen[..., None, :]).astype(BF16)


def gather_blocks(tokens, cotangent):
    return (lax.all_gather(tokens, "expert"), lax.all_gather(cotangent, "expert"))


def pick(table, blocks):
    picked = jnp.einsum("bst,btd->bsd", table, blocks, preferred_element_type=F32)
    return picked.reshape(-1, blocks.shape[-1])


def add_replicas(part, width):
    replicas = lax.axis_size("replica")
    me = lax.axis_index("replica")
    moved = []
    for step in range(1, replicas):
        to = lax.rem(me + step, replicas)
        ring = [(i, (i + step) % replicas) for i in range(replicas)]
        moved.append(lax.ppermute(part(to * width).astype(BF16), "replica", ring))
    total = part(me * width)
    for other in moved:
        total = total + other.astype(F32)
    return total


def send_back(rows, num_experts, capacity):
    moved = lax.all_to_all(
        rows.reshape(num_experts, capacity, rows.shape[1]), "expert", split_axis=0, concat_axis=0, tiled=True
    )
    return moved.reshape(num_experts * capacity, rows.shape[1])


def per_device(tokens, expert_ids, route_weights, w_gate, w_up, w_down, cotangent):
    num_experts = lax.axis_size("expert")
    tok_rows, top = expert_ids.shape
    capacity = tok_rows * top * 4 // (num_experts * 3)
    width = tokens.shape[1] // lax.axis_size("replica")
    me = lax.axis_index("expert")
    contract = (((1,), (1,)), ((), ()))

    routing = lax.all_gather(
        jnp.concatenate([expert_ids.astype(F32), route_weights], axis=1), "expert"
    )
    token_blocks, grad_blocks = gather_blocks(tokens, cotangent)
    mine = routing[:, :, :top] == me.astype(F32)
    table = slots_of(jnp.any(mine, axis=2), capacity)
    weight = jnp.sum(jnp.where(mine, routing[:, :, top:], 0.0), axis=2)
    slot_weight = jnp.sum(table.astype(F32) * weight[:, None, :], axis=2).reshape(-1, 1)
    own = expert_ids[None] == jnp.arange(num_experts, dtype=jnp.int32)[:, None, None]
    spread = slots_of(jnp.any(own, axis=2), capacity).reshape(num_experts * capacity, tok_rows)

    gate_w, up_w, down_w = w_gate[0], w_up[0], w_down[0]
    rows = pick(table, token_blocks).astype(BF16)
    gate = jnp.dot(rows, gate_w, preferred_element_type=F32)
    up = jnp.dot(rows, up_w, preferred_element_type=F32)
    sig = jax.nn.sigmoid(gate)
    act = gate * sig
    hidden = (act * up).astype(BF16)

    def forward_part(start):
        columns = lax.dynamic_slice_in_dim(down_w, start, width, 1)
        return jnp.dot(hidden, columns, preferred_element_type=F32)

    outputs = (add_replicas(forward_part, width) * slot_weight).astype(BF16)
    combine = (((0,), (0,)), ((), ()))
    mixed = lax.dot_general(
        spread, send_back(outputs, num_experts, capacity), combine, preferred_element_type=F32
    ).astype(BF16)

    grad_rows = (pick(table, grad_blocks) * slot_weight).astype(BF16)
    hidden_grad = lax.dot_general(grad_rows, down_w, contract, preferred_element_type=F32)
    gate_grad = (hidden_grad * up * sig * (1.0 + gate * (1.0 - sig))).astype(BF16)
    up_grad = (hidden_grad * act).astype(BF16)

    def backward_part(start):
        first = lax.dynamic_slice_in_dim(gate_w, start, width, 0)
        second = lax.dynamic_slice_in_dim(up_w, start, width, 0)
        return lax.dot_general(
            gate_grad, first, contract, preferred_element_type=F32
        ) + lax.dot_general(up_grad, second, contract, preferred_element_type=F32)

    returned = add_replicas(backward_part, width).astype(BF16)
    tokens_grad = lax.dot_general(
        spread, send_back(returned, num_experts, capacity), combine, preferred_element_type=F32
    ).astype(BF16)
    return (mixed, tokens_grad)


def solution(mesh):
    in_specs = (
        P("expert", None),
        P("expert", None),
        P("expert", None),
        P("expert", None, "replica"),
        P("expert", None, "replica"),
        P("expert", "replica", None),
        P("expert", None),
    )
    out_specs = (P("expert", "replica"), P("expert", "replica"))
    return jax.shard_map(
        per_device, mesh=mesh, in_specs=in_specs, out_specs=out_specs, check_vma=False
    )
```

```python
import jax
import jax.numpy as jnp
from jax import lax
from jax.sharding import PartitionSpec as P

BF16 = jnp.bfloat16
F32 = jnp.float32


def slots_of(chosen, capacity):
    count = chosen.shape[-1]
    earlier = (jnp.arange(count)[:, None] < jnp.arange(count)[None, :]).astype(BF16)
    slot = jnp.dot(chosen.astype(BF16), earlier, preferred_element_type=F32).astype(jnp.int32)
    at_slot = slot[..., None, :] == jnp.arange(capacity, dtype=jnp.int32)[:, None]
    return (at_slot & chosen[..., None, :]).astype(BF16)


def gather_blocks(tokens, cotangent):
    return (lax.all_gather(tokens, "expert"), lax.all_gather(cotangent, "expert"))


def pick(table, blocks):
    picked = jnp.einsum("bst,btd->bsd", table, blocks, preferred_element_type=F32)
    return picked.reshape(-1, blocks.shape[-1])


def add_replicas(part, width, offset=0, after=None):
    replicas = lax.axis_size("replica")
    me = lax.axis_index("replica")
    moved = []
    for step in range(1, replicas):
        to = lax.rem(me + step, replicas)
        ring = [(i, (i + step) % replicas) for i in range(replicas)]
        term = part(to * width + offset).astype(BF16)
        if after is not None:
            term, _ = lax.optimization_barrier((term, after))
        moved.append(lax.ppermute(term, "replica", ring))
    total = part(me * width + offset)
    for other in moved:
        total = total + other.astype(F32)
    return (total, moved)


def send_back(rows, num_experts, capacity):
    moved = lax.all_to_all(
        rows.reshape(num_experts, capacity, rows.shape[1]), "expert", split_axis=0, concat_axis=0, tiled=True
    )
    return moved.reshape(num_experts * capacity, rows.shape[1])


def per_device(tokens, expert_ids, route_weights, w_gate, w_up, w_down, cotangent):
    num_experts = lax.axis_size("expert")
    tok_rows, top = expert_ids.shape
    capacity = tok_rows * top * 4 // (num_experts * 3)
    width = tokens.shape[1] // lax.axis_size("replica")
    me = lax.axis_index("expert")
    contract = (((1,), (1,)), ((), ()))

    routing = lax.all_gather(
        jnp.concatenate([expert_ids.astype(F32), route_weights], axis=1), "expert"
    )
    token_blocks, grad_blocks = gather_blocks(tokens, cotangent)
    mine = routing[:, :, :top] == me.astype(F32)
    table = slots_of(jnp.any(mine, axis=2), capacity)
    weight = jnp.sum(jnp.where(mine, routing[:, :, top:], 0.0), axis=2)
    slot_weight = jnp.sum(table.astype(F32) * weight[:, None, :], axis=2).reshape(-1, 1)
    own = expert_ids[None] == jnp.arange(num_experts, dtype=jnp.int32)[:, None, None]
    spread = slots_of(jnp.any(own, axis=2), capacity).reshape(num_experts * capacity, tok_rows)

    gate_w, up_w, down_w = w_gate[0], w_up[0], w_down[0]
    rows = pick(table, token_blocks).astype(BF16)
    gate = jnp.dot(rows, gate_w, preferred_element_type=F32)
    up = jnp.dot(rows, up_w, preferred_element_type=F32)
    sig = jax.nn.sigmoid(gate)
    act = gate * sig
    hidden = (act * up).astype(BF16)

    def forward_part(start):
        columns = lax.dynamic_slice_in_dim(down_w, start, width, 1)
        return jnp.dot(hidden, columns, preferred_element_type=F32)

    outputs = (add_replicas(forward_part, width)[0] * slot_weight).astype(BF16)
    grad_blocks, outputs = lax.optimization_barrier((grad_blocks, outputs))
    combine = (((0,), (0,)), ((), ()))
    mixed = lax.dot_general(
        spread, send_back(outputs, num_experts, capacity), combine, preferred_element_type=F32
    ).astype(BF16)

    grad_rows = (pick(table, grad_blocks) * slot_weight).astype(BF16)
    hidden_grad = lax.dot_general(grad_rows, down_w, contract, preferred_element_type=F32)
    gate_grad = (hidden_grad * up * sig * (1.0 + gate * (1.0 - sig))).astype(BF16)
    up_grad = (hidden_grad * act).astype(BF16)

    pieces = 2
    piece = width // pieces

    def backward_part(start):
        first = lax.dynamic_slice_in_dim(gate_w, start, piece, 0)
        second = lax.dynamic_slice_in_dim(up_w, start, piece, 0)
        return lax.dot_general(
            gate_grad, first, contract, preferred_element_type=F32
        ) + lax.dot_general(up_grad, second, contract, preferred_element_type=F32)

    columns, crossed = [], None
    for at in range(pieces):
        total, crossed = add_replicas(backward_part, width, at * piece, crossed)
        total = total.astype(BF16)
        if at == 0:
            total, mixed, crossed = lax.optimization_barrier((total, mixed, crossed))
        returned = send_back(total, num_experts, capacity)
        columns.append(
            lax.dot_general(spread, returned, combine, preferred_element_type=F32).astype(BF16)
        )
    tokens_grad = jnp.concatenate(columns, axis=1)
    return (mixed, tokens_grad)


def solution(mesh):
    in_specs = (
        P("expert", None),
        P("expert", None),
        P("expert", None),
        P("expert", None, "replica"),
        P("expert", None, "replica"),
        P("expert", "replica", None),
        P("expert", None),
    )
    out_specs = (P("expert", "replica"), P("expert", "replica"))
    return jax.shard_map(
        per_device, mesh=mesh, in_specs=in_specs, out_specs=out_specs, check_vma=False
    )
```
